32 devices in a mesh: gx: 2 (over x), gy: 4 (over y, core), gz: 4 (over z).
Axes of the slice: x: 2, y: 2, z: 4, core: 2. Of those that a mesh axis runs over, the one named last changes fastest.
Arguments:
- normed: bfloat16 [4096, 3072], P(('gy', 'gx'), 'gz'), may hold values from -6 to 6
- out_grad: bfloat16 [4096, 3072], P(('gy', 'gx'), 'gz'), may hold values from -6 to 6
- projected: bfloat16 [4096, 9216], P('gy', 'gx'), may hold values from -5 to 5
- mixed_heads: bfloat16 [4096, 3072], P('gy', 'gx'), may hold values from -6 to 6
- hidden_pre: bfloat16 [4096, 12288], P('gy', 'gx'), may hold values from -6 to 6
- attend_in: bfloat16 [3072, 9216], P('gz', ('gx', 'gy')), may hold values from -0.109375 to 0.109375
- hidden_in: bfloat16 [3072, 12288], P('gz', ('gx', 'gy')), may hold values from -0.109375 to 0.109375
- attend_out: bfloat16 [3072, 3072], P(('gx', 'gy'), 'gz'), may hold values from -0.109375 to 0.109375
- hidden_out: bfloat16 [12288, 3072], P(('gx', 'gy'), 'gz'), may hold values from -0.0546875 to 0.0546875
Outputs:
- normed_grad: bfloat16 [4096, 3072], P(('gy', 'gx'), 'gz')
- attend_in_grad: bfloat16 [3072, 9216], P('gz', ('gx', 'gy'))
- hidden_in_grad: bfloat16 [3072, 12288], P('gz', ('gx', 'gy'))
- attend_out_grad: bfloat16 [3072, 3072], P(('gx', 'gy'), 'gz')
- hidden_out_grad: bfloat16 [12288, 3072], P(('gx', 'gy'), 'gz')
The draws below stay inside these ranges and needn't reach their ends.
All inputs are finite; a program needn't handle non-finite values.
Results may differ from the reference program's by a relative error of at most 0.02.
Values may be sent and summed in bfloat16 or wider, within the bound.
A program may use at most 256 MiB of HBM per device.

```python
import jax
import jax.numpy as jnp
from jax import lax

D = 3072
HEADS = 24
HEAD = 128
FF = 12288
LEN = 1024
IMAGES = 4
TOKENS = 4096
DA = 3072


def draw_projected(key, part):
    key = jax.random.fold_in(key, 11)
    first_key = jax.random.fold_in(key, 0)
    stacked = jnp.clip(jax.random.normal(first_key, (TOKENS, HEADS, 3, HEAD), jnp.float32), -5.0, 5.0)
    return stacked.reshape(TOKENS, 3 * HEADS * HEAD).astype(jnp.bfloat16)


def level_of(own_key, extent, cuts, low, high):
    def one(dim, parts):
        draws = jax.random.uniform(jax.random.fold_in(jax.random.fold_in(own_key, 6), dim), (parts,), jnp.float32, low / len(cuts), high / len(cuts))
        return jnp.repeat(jnp.exp(draws), extent[dim] // parts).reshape((-1,) + (1,) * (len(extent) - dim - 1))

    gain = one(*cuts[0])
    for cut in cuts[1:]:
        gain = gain * one(*cut)
    return gain


def normal_values(stream_key, shape, width, most, shards=(), kind=jnp.bfloat16):
    drawn = jax.random.normal(stream_key, shape, jnp.float32) * width
    if len(shards) > 0:
        drawn = level_of(stream_key, shape, shards, -0.22, 0.18) * drawn
    return jnp.clip(drawn, min=-most, max=most).astype(kind)


def setup_inputs(seed: int = 0) -> dict:
    key_of = jax.random.split(jax.random.key(seed), 10)
    return {
        "normed": normal_values(key_of[0], (TOKENS, D), 1.0, 6.0, ((0, 8), (1, 4))),
        "out_grad": normal_values(key_of[1], (TOKENS, D), 1.0, 6.0, ((0, 8), (1, 4))),
        "projected": draw_projected(jax.random.fold_in(key_of[9], 71), 0),
        "mixed_heads": normal_values(key_of[3], (TOKENS, DA), 1.0, 6.0, ((0, 4), (1, 2))),
        "hidden_pre": normal_values(key_of[4], (TOKENS, FF), 1.0, 6.0, ((0, 4), (1, 2))),
        "attend_in": normal_values(key_of[5], (D, 3 * DA), D ** -0.5, 0.109375, ((0, 4), (1, 8))),
        "hidden_in": normal_values(key_of[6], (D, FF), D ** -0.5, 0.109375, ((0, 4), (1, 8))),
        "attend_out": normal_values(key_of[7], (DA, D), DA ** -0.5, 0.109375, ((0, 8), (1, 4))),
        "hidden_out": normal_values(key_of[8], (FF, D), FF ** -0.5, 0.0546875, ((0, 8), (1, 4))),
    }


def gelu_value(values):
    return 0.5 * values * (1.0 + lax.erf(values * 0.7071067811865476))


def gelu_slope(values):
    return 0.5 * (1.0 + lax.erf(values * 0.7071067811865476)) + values * jnp.exp(-0.5 * values * values) * 0.3989422804014327


def head_backward(inputs):
    queries, key_rows, value_rows, head_grad = inputs
    score_scale = HEAD ** -0.5
    scores = jnp.dot(queries, key_rows.T, preferred_element_type=jnp.float32) * score_scale
    largest = jnp.max(scores, axis=1, keepdims=True)
    weights = jnp.exp(scores - largest)
    probability = weights / jnp.sum(weights, axis=1, keepdims=True)
    value_grad = jnp.dot(probability.astype(jnp.bfloat16).T, head_grad, preferred_element_type=jnp.float32)
    prob_grad = jnp.dot(head_grad, value_rows.T, preferred_element_type=jnp.float32)
    centre = jnp.sum(probability * prob_grad, axis=1, keepdims=True)
    score_grad = (probability * (prob_grad - centre)).astype(jnp.bfloat16)
    query_grad = score_scale * jnp.dot(score_grad, key_rows, preferred_element_type=jnp.float32)
    key_grad = score_scale * jnp.dot(score_grad.T, queries, preferred_element_type=jnp.float32)
    return jnp.stack([query_grad, key_grad, value_grad], axis=1)


def reference(normed, out_grad, projected, mixed_heads, hidden_pre, attend_in, hidden_in, attend_out, hidden_out):
    merge_part = jnp.dot(out_grad, attend_out.T, preferred_element_type=jnp.float32)
    hidden_part = jnp.dot(out_grad, hidden_out.T, preferred_element_type=jnp.float32)
    heads_grad = merge_part.astype(jnp.bfloat16)
    pre_float = hidden_pre.astype(jnp.float32)
    hidden_grad = (hidden_part * gelu_slope(pre_float)).astype(jnp.bfloat16)
    activated = gelu_value(pre_float).astype(jnp.bfloat16)
    split_heads = projected.reshape(IMAGES, LEN, HEADS, 3, HEAD).transpose(2, 0, 3, 1, 4).reshape(
        HEADS * IMAGES, 3, LEN, HEAD)
    grads_heads = heads_grad.reshape(IMAGES, LEN, HEADS, HEAD).transpose(2, 0, 1, 3).reshape(
        HEADS * IMAGES, LEN, HEAD)
    stacked = lax.map(head_backward, (split_heads[:, 0], split_heads[:, 1], split_heads[:, 2], grads_heads))
    projected_grad = stacked.reshape(HEADS, IMAGES, LEN, 3, HEAD).transpose(1, 2, 0, 3, 4).reshape(
        TOKENS, 3 * DA).astype(jnp.bfloat16)
    normed_grad = (jnp.dot(projected_grad, attend_in.T, preferred_element_type=jnp.float32)
                   + jnp.dot(hidden_grad, hidden_in.T, preferred_element_type=jnp.float32)).astype(jnp.bfloat16)
    attend_in_grad = jnp.dot(normed.T, projected_grad, preferred_element_type=jnp.float32).astype(jnp.bfloat16)
    hidden_in_grad = jnp.dot(normed.T, hidden_grad, preferred_element_type=jnp.float32).astype(jnp.bfloat16)
    attend_out_grad = jnp.dot(mixed_heads.T, out_grad, preferred_element_type=jnp.float32).astype(jnp.bfloat16)
    hidden_out_grad = jnp.dot(activated.T, out_grad, preferred_element_type=jnp.float32).astype(jnp.bfloat16)
    return (normed_grad, attend_in_grad, hidden_in_grad, attend_out_grad, hidden_out_grad)
```

```python
import jax
import jax.numpy as jnp
from jax import lax
from jax.experimental import pallas as pl
from jax.experimental.pallas import tpu as pltpu
from jax.sharding import PartitionSpec as P

HEAD = 128
LEN = 1024


def gelu_value(values):
    return 0.5 * values * (1.0 + lax.erf(values * 0.7071067811865476))


def gelu_slope(values):
    return (
        0.5 * (1.0 + lax.erf(values * 0.7071067811865476))
        + values * jnp.exp(-0.5 * values * values) * 0.3989422804014327
    )


def local(
    normed,
    out_grad,
    projected,
    mixed_heads,
    hidden_pre,
    attend_in,
    hidden_in,
    attend_out,
    hidden_out,
):
    slab_count = projected.shape[0]
    depth = lax.axis_size("gz")
    block = slab_count // depth
    offset = lax.axis_index("gz") * block
    normed_slab, grad_slab = (
        lax.all_gather(normed, "gx", axis=0, tiled=True),
        lax.all_gather(out_grad, "gx", axis=0, tiled=True),
    )
    attend_cols, hidden_cols, attend_rows, hidden_rows = (
        lax.all_gather(attend_in, "gy", axis=1, tiled=True),
        lax.all_gather(hidden_in, "gy", axis=1, tiled=True),
        lax.all_gather(attend_out, "gy", axis=0, tiled=True),
        lax.all_gather(hidden_out, "gy", axis=0, tiled=True),
    )
    merge_part = jnp.einsum("td,gd->tg", grad_slab, attend_rows, preferred_element_type=jnp.float32)
    hidden_part = jnp.einsum(
        "td,gd->tg", grad_slab, hidden_rows, preferred_element_type=jnp.float32
    )
    pre_float = hidden_pre.astype(jnp.float32)
    merge_rows, hidden_sum = (
        lax.psum_scatter(merge_part, "gz", scatter_dimension=0, tiled=True),
        lax.psum_scatter(hidden_part, "gz", scatter_dimension=0, tiled=True),
    )
    slope_rows = gelu_slope(lax.dynamic_slice_in_dim(pre_float, offset, block, 0))
    hidden_grad_rows = (hidden_sum * slope_rows).astype(jnp.bfloat16)
    heads_grad = merge_rows.astype(jnp.bfloat16)
    heads_here = projected.shape[1] // (3 * HEAD)
    score_scale = HEAD ** (-0.5)
    span = max(block, LEN)
    keyed = projected.reshape(slab_count, heads_here, 3, HEAD)
    local_rows = lax.dynamic_slice_in_dim(keyed, offset, block, 0)
    queries = local_rows[:, :, 0]
    key_rows = keyed[:, :, 1]
    value_rows = keyed[:, :, 2]
    head_grad = heads_grad.reshape(block, heads_here, HEAD)
    scores = (
        jnp.einsum("qhd,khd->hqk", queries, key_rows, preferred_element_type=jnp.float32)
        * score_scale
    )
    largest = jnp.max(scores, axis=2, keepdims=True)
    weights = jnp.exp(scores - largest)
    probability = weights / jnp.sum(weights, axis=2, keepdims=True)
    value_grad = jnp.einsum(
        "hqk,qhd->khd",
        probability.astype(jnp.bfloat16),
        head_grad,
        preferred_element_type=jnp.float32,
    )
    prob_grad = jnp.einsum(
        "qhd,khd->hqk", head_grad, value_rows, preferred_element_type=jnp.float32
    )
    centre = jnp.sum(probability * prob_grad, axis=2, keepdims=True)
    score_grad = (probability * (prob_grad - centre)).astype(jnp.bfloat16)
    query_grad = score_scale * jnp.einsum(
        "hqk,khd->qhd", score_grad, key_rows, preferred_element_type=jnp.float32
    )
    key_grad = score_scale * jnp.einsum(
        "hqk,qhd->khd", score_grad, queries, preferred_element_type=jnp.float32
    )
    key_value = jnp.stack([key_grad, value_grad], axis=2).reshape(span, heads_here * 2 * HEAD)
    summed = (
        lax.psum_scatter(key_value.astype(jnp.bfloat16), "gz", scatter_dimension=0, tiled=True)
        .astype(jnp.float32)
        .reshape(block, heads_here, 2, HEAD)
    )
    projected_grad_rows = (
        jnp.concatenate([query_grad[:, :, None], summed], axis=2)
        .reshape(block, 3 * heads_here * HEAD)
        .astype(jnp.bfloat16)
    )
    projected_grad, hidden_grad = (
        lax.all_gather(projected_grad_rows, "gz", axis=0, tiled=True),
        lax.all_gather(hidden_grad_rows, "gz", axis=0, tiled=True),
    )
    local_grad = jnp.einsum(
        "tq,dq->td", projected_grad, attend_cols, preferred_element_type=jnp.float32
    ) + jnp.einsum("tq,dq->td", hidden_grad, hidden_cols, preferred_element_type=jnp.float32)
    normed_grad = lax.psum_scatter(
        local_grad.astype(jnp.bfloat16), "gx", scatter_dimension=0, tiled=True
    )
    activated = gelu_value(pre_float).astype(jnp.bfloat16)
    part_attend_in = jnp.einsum(
        "td,tq->dq", normed_slab, projected_grad, preferred_element_type=jnp.float32
    )
    part_hidden_in = jnp.einsum(
        "td,tq->dq", normed_slab, hidden_grad, preferred_element_type=jnp.float32
    )
    part_attend_out = jnp.einsum(
        "tg,td->gd", mixed_heads, grad_slab, preferred_element_type=jnp.float32
    )
    part_hidden_out = jnp.einsum(
        "tg,td->gd", activated, grad_slab, preferred_element_type=jnp.float32
    )
    sum_attend_in, sum_hidden_in, sum_attend_out, sum_hidden_out = (
        lax.psum_scatter(
            part_attend_in.astype(jnp.bfloat16), "gy", scatter_dimension=1, tiled=True
        ).astype(jnp.float32),
        lax.psum_scatter(
            part_hidden_in.astype(jnp.bfloat16), "gy", scatter_dimension=1, tiled=True
        ).astype(jnp.float32),
        lax.psum_scatter(
            part_attend_out.astype(jnp.bfloat16), "gy", scatter_dimension=0, tiled=True
        ).astype(jnp.float32),
        lax.psum_scatter(
            part_hidden_out.astype(jnp.bfloat16), "gy", scatter_dimension=0, tiled=True
        ).astype(jnp.float32),
    )
    return (
        normed_grad,
        sum_attend_in.astype(jnp.bfloat16),
        sum_hidden_in.astype(jnp.bfloat16),
        sum_attend_out.astype(jnp.bfloat16),
        sum_hidden_out.astype(jnp.bfloat16),
    )


SWAP = (0, 2, 1, 3)


def attention_kernel(keyed_ref, grad_ref, out_ref):
    score_scale = HEAD ** (-0.5)
    across = (((1,), (1,)), ((), ()))
    along = (((0,), (0,)), ((), ()))
    keys = keyed_ref[:, HEAD : 2 * HEAD]
    values = keyed_ref[:, 2 * HEAD :]
    count = keyed_ref.shape[0]
    step = min(256, count)
    key_grad = jnp.zeros((count, HEAD), jnp.float32)
    value_grad = jnp.zeros((count, HEAD), jnp.float32)
    for start in range(0, count, step):
        rows = slice(start, start + step)
        queries = keyed_ref[rows, :HEAD]
        grads = grad_ref[rows, :]
        scores = (
            lax.dot_general(queries, keys, across, preferred_element_type=jnp.float32)
            * score_scale
        )
        weights = jnp.exp(scores - jnp.max(scores, axis=1, keepdims=True))
        probability = weights / jnp.sum(weights, axis=1, keepdims=True)
        prob_grad = lax.dot_general(grads, values, across, preferred_element_type=jnp.float32)
        centre = jnp.sum(probability * prob_grad, axis=1, keepdims=True)
        score_grad = (probability * (prob_grad - centre)).astype(jnp.bfloat16)
        query_grad = score_scale * jnp.dot(score_grad, keys, preferred_element_type=jnp.float32)
        out_ref[rows, :HEAD] = query_grad.astype(jnp.bfloat16)
        key_grad += lax.dot_general(
            score_grad, queries, along, preferred_element_type=jnp.float32
        )
        value_grad += lax.dot_general(
            probability.astype(jnp.bfloat16), grads, along, preferred_element_type=jnp.float32
        )
    out_ref[:, HEAD : 2 * HEAD] = (score_scale * key_grad).astype(jnp.bfloat16)
    out_ref[:, 2 * HEAD :] = value_grad.astype(jnp.bfloat16)


def attention_backward(keyed, head_grad):
    count = keyed.shape[0]
    heads = keyed.shape[1] // (3 * HEAD)
    return pl.pallas_call(
        attention_kernel,
        grid=(heads,),
        in_specs=[
            pl.BlockSpec((count, 3 * HEAD), lambda head: (0, head)),
            pl.BlockSpec((count, HEAD), lambda head: (0, head)),
        ],
        out_specs=pl.BlockSpec((count, 3 * HEAD), lambda head: (0, head)),
        out_shape=jax.ShapeDtypeStruct(keyed.shape, jnp.bfloat16),
        compiler_params=pltpu.CompilerParams(vmem_limit_bytes=40 * 1024 * 1024),
        cost_estimate=pl.CostEstimate(
            flops=10 * heads * count * count * HEAD,
            bytes_accessed=14 * heads * count * HEAD,
            transcendentals=heads * count * count,
        ),
    )(keyed, head_grad)


def exchange(block, axis, flip):
    size = lax.axis_size(axis)
    return lax.ppermute(block, axis, [(i, i ^ flip) for i in range(size)])


def turn(block):
    pairs = [
        (g * 4 + z, SWAP[z] * 4 + SWAP[g]) for g in range(4) for z in range(4)
    ]
    return lax.ppermute(block, ("gy", "gz"), pairs)


def gather_width(block, dim):
    place = lax.axis_index("gy")
    width = block.shape[dim]
    shape = list(block.shape)
    shape[dim] = 4 * width
    whole = jnp.zeros(tuple(shape), block.dtype)
    beside = exchange(block, "gy", 1)
    opposite = exchange(block, "gy", 2)
    last = exchange(opposite, "gy", 1)
    for flip, part in ((0, block), (1, beside), (2, opposite), (3, last)):
        whole = lax.dynamic_update_slice_in_dim(
            whole, part, lax.bitwise_xor(place, flip) * width, dim
        )
    return whole


def both_halves(half):
    other = exchange(half, "gx", 1)
    first = lax.axis_index("gx") == 0
    return jnp.concatenate([jnp.where(first, half, other), jnp.where(first, other, half)], axis=0)


def whole_width(rows):
    blocks = lax.all_gather(rows, "gz", axis=0)
    return jnp.concatenate([blocks[SWAP[i]] for i in range(4)], axis=1)


def local_columns(
    normed,
    out_grad,
    projected,
    mixed_heads,
    hidden_pre,
    attend_in,
    hidden_in,
    attend_out,
    hidden_out,
):
    side = lax.axis_index("gx")
    deep = lax.axis_index("gz")
    column = 2 * lax.rem(deep, 2) + deep // 2
    half = normed.shape[0]
    grad_own = both_halves(out_grad)
    grad_slab = both_halves(whole_width(out_grad))
    attend_rows = gather_width(turn(attend_out), 1)
    hidden_rows = gather_width(turn(hidden_out), 1)
    normed_slab = both_halves(whole_width(normed))
    attend_cols = gather_width(turn(attend_in), 0)
    hidden_cols = gather_width(turn(hidden_in), 0)

    activated = gelu_value(hidden_pre.astype(jnp.float32)).astype(jnp.bfloat16)
    part_attend_out = jnp.einsum(
        "tg,td->gd", mixed_heads, grad_own, preferred_element_type=jnp.float32
    ).astype(jnp.bfloat16)
    part_hidden_out = jnp.einsum(
        "tg,td->gd", activated, grad_own, preferred_element_type=jnp.float32
    ).astype(jnp.bfloat16)
    attend_out_grad = lax.psum_scatter(part_attend_out, "gy", scatter_dimension=0, tiled=True)
    hidden_out_grad = lax.psum_scatter(part_hidden_out, "gy", scatter_dimension=0, tiled=True)

    head_grad = jnp.einsum(
        "td,gd->tg", grad_slab, attend_rows, preferred_element_type=jnp.float32
    ).astype(jnp.bfloat16)
    width = attend_in.shape[1]
    keyed = lax.dynamic_slice_in_dim(projected, column * width, width, 1)
    projected_grad = attention_backward(keyed, head_grad)

    units = hidden_in.shape[1]
    pre_here = lax.dynamic_slice_in_dim(hidden_pre, column * units, units, 1)
    hidden_part = jnp.einsum(
        "td,gd->tg", grad_slab, hidden_rows, preferred_element_type=jnp.float32
    )
    hidden_grad = (hidden_part * gelu_slope(pre_here.astype(jnp.float32))).astype(jnp.bfloat16)

    part_attend_in = jnp.einsum(
        "td,tq->dq", normed_slab, projected_grad, preferred_element_type=jnp.float32
    ).astype(jnp.bfloat16)
    part_hidden_in = jnp.einsum(
        "td,tq->dq", normed_slab, hidden_grad, preferred_element_type=jnp.float32
    ).astype(jnp.bfloat16)
    attend_in_grad = turn(lax.psum_scatter(part_attend_in, "gy", scatter_dimension=0, tiled=True))
    hidden_in_grad = turn(lax.psum_scatter(part_hidden_in, "gy", scatter_dimension=0, tiled=True))

    def input_grad(start):
        attend_part = lax.dynamic_slice_in_dim(projected_grad, start, half, 0)
        hidden_part = lax.dynamic_slice_in_dim(hidden_grad, start, half, 0)
        return jnp.einsum(
            "tq,dq->td", attend_part, attend_cols, preferred_element_type=jnp.float32
        ) + jnp.einsum("tq,dq->td", hidden_part, hidden_cols, preferred_element_type=jnp.float32)

    arrived = exchange(input_grad((1 - side) * half).astype(jnp.bfloat16), "gx", 1)
    row_grad = (input_grad(side * half) + arrived.astype(jnp.float32)).astype(jnp.bfloat16)
    block = normed.shape[1]
    row_grad = jnp.concatenate(
        [row_grad[:, SWAP[i] * block : (SWAP[i] + 1) * block] for i in range(4)], axis=1
    )
    normed_grad = lax.psum_scatter(row_grad, "gz", scatter_dimension=1, tiled=True)
    return normed_grad, attend_in_grad, hidden_in_grad, attend_out_grad, hidden_out_grad


def chosen(*arrays):
    normed, projected, attend_in = arrays[0], arrays[2], arrays[5]
    sizes = tuple(lax.axis_size(axis) for axis in ("gx", "gy", "gz"))
    fits = (
        sizes == (2, 4, 4)
        and projected.shape[0] == LEN
        and attend_in.shape[1] % (3 * HEAD) == 0
        and normed.shape[0] * 2 == LEN
    )
    return (local_columns if fits else local)(*arrays)


def solution(mesh):
    placed = (
        P(("gy", "gx"), "gz"),
        P(("gy", "gx"), "gz"),
        P("gy", "gx"),
        P("gy", "gx"),
        P("gy", "gx"),
        P("gz", ("gx", "gy")),
        P("gz", ("gx", "gy")),
        P(("gx", "gy"), "gz"),
        P(("gx", "gy"), "gz"),
    )
    return jax.shard_map(
        chosen,
        mesh=mesh,
        in_specs=placed,
        out_specs=(
            P(("gy", "gx"), "gz"),
            P("gz", ("gx", "gy")),
            P("gz", ("gx", "gy")),
            P(("gx", "gy"), "gz"),
            P(("gx", "gy"), "gz"),
        ),
        check_vma=False,
    )
```

```python
import jax
import jax.numpy as jnp
from jax import lax
from jax.experimental import pallas as pl
from jax.experimental.pallas import tpu as pltpu
from jax.sharding import PartitionSpec as P

HEAD = 128
LEN = 1024


def gelu_value(values):
    return 0.5 * values * (1.0 + lax.erf(values * 0.7071067811865476))


def gelu_slope(values):
    return (
        0.5 * (1.0 + lax.erf(values * 0.7071067811865476))
        + values * jnp.exp(-0.5 * values * values) * 0.3989422804014327
    )


def local(
    normed,
    out_grad,
    projected,
    mixed_heads,
    hidden_pre,
    attend_in,
    hidden_in,
    attend_out,
    hidden_out,
):
    slab_count = projected.shape[0]
    depth = lax.axis_size("gz")
    block = slab_count // depth
    offset = lax.axis_index("gz") * block
    normed_slab, grad_slab = (
        lax.all_gather(normed, "gx", axis=0, tiled=True),
        lax.all_gather(out_grad, "gx", axis=0, tiled=True),
    )
    attend_cols, hidden_cols, attend_rows, hidden_rows = (
        lax.all_gather(attend_in, "gy", axis=1, tiled=True),
        lax.all_gather(hidden_in, "gy", axis=1, tiled=True),
        lax.all_gather(attend_out, "gy", axis=0, tiled=True),
        lax.all_gather(hidden_out, "gy", axis=0, tiled=True),
    )
    merge_part = jnp.einsum("td,gd->tg", grad_slab, attend_rows, preferred_element_type=jnp.float32)
    hidden_part = jnp.einsum(
        "td,gd->tg", grad_slab, hidden_rows, preferred_element_type=jnp.float32
    )
    pre_float = hidden_pre.astype(jnp.float32)
    merge_rows, hidden_sum = (
        lax.psum_scatter(merge_part, "gz", scatter_dimension=0, tiled=True),
        lax.psum_scatter(hidden_part, "gz", scatter_dimension=0, tiled=True),
    )
    slope_rows = gelu_slope(lax.dynamic_slice_in_dim(pre_float, offset, block, 0))
    hidden_grad_rows = (hidden_sum * slope_rows).astype(jnp.bfloat16)
    heads_grad = merge_rows.astype(jnp.bfloat16)
    heads_here = projected.shape[1] // (3 * HEAD)
    score_scale = HEAD ** (-0.5)
    span = max(block, LEN)
    keyed = projected.reshape(slab_count, heads_here, 3, HEAD)
    local_rows = lax.dynamic_slice_in_dim(keyed, offset, block, 0)
    queries = local_rows[:, :, 0]
    key_rows = keyed[:, :, 1]
    value_rows = keyed[:, :, 2]
    head_grad = heads_grad.reshape(block, heads_here, HEAD)
    scores = (
        jnp.einsum("qhd,khd->hqk", queries, key_rows, preferred_element_type=jnp.float32)
        * score_scale
    )
    largest = jnp.max(scores, axis=2, keepdims=True)
    weights = jnp.exp(scores - largest)
    probability = weights / jnp.sum(weights, axis=2, keepdims=True)
    value_grad = jnp.einsum(
        "hqk,qhd->khd",
        probability.astype(jnp.bfloat16),
        head_grad,
        preferred_element_type=jnp.float32,
    )
    prob_grad = jnp.einsum(
        "qhd,khd->hqk", head_grad, value_rows, preferred_element_type=jnp.float32
    )
    centre = jnp.sum(probability * prob_grad, axis=2, keepdims=True)
    score_grad = (probability * (prob_grad - centre)).astype(jnp.bfloat16)
    query_grad = score_scale * jnp.einsum(
        "hqk,khd->qhd", score_grad, key_rows, preferred_element_type=jnp.float32
    )
    key_grad = score_scale * jnp.einsum(
        "hqk,qhd->khd", score_grad, queries, preferred_element_type=jnp.float32
    )
    key_value = jnp.stack([key_grad, value_grad], axis=2).reshape(span, heads_here * 2 * HEAD)
    summed = (
        lax.psum_scatter(key_value.astype(jnp.bfloat16), "gz", scatter_dimension=0, tiled=True)
        .astype(jnp.float32)
        .reshape(block, heads_here, 2, HEAD)
    )
    projected_grad_rows = (
        jnp.concatenate([query_grad[:, :, None], summed], axis=2)
        .reshape(block, 3 * heads_here * HEAD)
        .astype(jnp.bfloat16)
    )
    projected_grad, hidden_grad = (
        lax.all_gather(projected_grad_rows, "gz", axis=0, tiled=True),
        lax.all_gather(hidden_grad_rows, "gz", axis=0, tiled=True),
    )
    local_grad = jnp.einsum(
        "tq,dq->td", projected_grad, attend_cols, preferred_element_type=jnp.float32
    ) + jnp.einsum("tq,dq->td", hidden_grad, hidden_cols, preferred_element_type=jnp.float32)
    normed_grad = lax.psum_scatter(
        local_grad.astype(jnp.bfloat16), "gx", scatter_dimension=0, tiled=True
    )
    activated = gelu_value(pre_float).astype(jnp.bfloat16)
    part_attend_in = jnp.einsum(
        "td,tq->dq", normed_slab, projected_grad, preferred_element_type=jnp.float32
    )
    part_hidden_in = jnp.einsum(
        "td,tq->dq", normed_slab, hidden_grad, preferred_element_type=jnp.float32
    )
    part_attend_out = jnp.einsum(
        "tg,td->gd", mixed_heads, grad_slab, preferred_element_type=jnp.float32
    )
    part_hidden_out = jnp.einsum(
        "tg,td->gd", activated, grad_slab, preferred_element_type=jnp.float32
    )
    sum_attend_in, sum_hidden_in, sum_attend_out, sum_hidden_out = (
        lax.psum_scatter(
            part_attend_in.astype(jnp.bfloat16), "gy", scatter_dimension=1, tiled=True
        ).astype(jnp.float32),
        lax.psum_scatter(
            part_hidden_in.astype(jnp.bfloat16), "gy", scatter_dimension=1, tiled=True
        ).astype(jnp.float32),
        lax.psum_scatter(
            part_attend_out.astype(jnp.bfloat16), "gy", scatter_dimension=0, tiled=True
        ).astype(jnp.float32),
        lax.psum_scatter(
            part_hidden_out.astype(jnp.bfloat16), "gy", scatter_dimension=0, tiled=True
        ).astype(jnp.float32),
    )
    return (
        normed_grad,
        sum_attend_in.astype(jnp.bfloat16),
        sum_hidden_in.astype(jnp.bfloat16),
        sum_attend_out.astype(jnp.bfloat16),
        sum_hidden_out.astype(jnp.bfloat16),
    )


SWAP = (0, 2, 1, 3)


def attention_kernel(keyed_ref, grad_ref, out_ref):
    score_scale = HEAD ** (-0.5)
    across = (((1,), (1,)), ((), ()))
    along = (((0,), (0,)), ((), ()))
    keys = keyed_ref[:, HEAD : 2 * HEAD]
    values = keyed_ref[:, 2 * HEAD :]
    count = keyed_ref.shape[0]
    step = min(256, count)
    key_grad = jnp.zeros((count, HEAD), jnp.float32)
    value_grad = jnp.zeros((count, HEAD), jnp.float32)
    for start in range(0, count, step):
        rows = slice(start, start + step)
        queries = keyed_ref[rows, :HEAD]
        grads = grad_ref[rows, :]
        scores = (
            lax.dot_general(queries, keys, across, preferred_element_type=jnp.float32)
            * score_scale
        )
        weights = jnp.exp(scores - jnp.max(scores, axis=1, keepdims=True))
        probability = weights / jnp.sum(weights, axis=1, keepdims=True)
        prob_grad = lax.dot_general(grads, values, across, preferred_element_type=jnp.float32)
        centre = jnp.sum(probability * prob_grad, axis=1, keepdims=True)
        score_grad = (probability * (prob_grad - centre)).astype(jnp.bfloat16)
        query_grad = score_scale * jnp.dot(score_grad, keys, preferred_element_type=jnp.float32)
        out_ref[rows, :HEAD] = query_grad.astype(jnp.bfloat16)
        key_grad += lax.dot_general(
            score_grad, queries, along, preferred_element_type=jnp.float32
        )
        value_grad += lax.dot_general(
            probability.astype(jnp.bfloat16), grads, along, preferred_element_type=jnp.float32
        )
    out_ref[:, HEAD : 2 * HEAD] = (score_scale * key_grad).astype(jnp.bfloat16)
    out_ref[:, 2 * HEAD :] = value_grad.astype(jnp.bfloat16)


def attention_backward(keyed, head_grad):
    count = keyed.shape[0]
    heads = keyed.shape[1] // (3 * HEAD)
    return pl.pallas_call(
        attention_kernel,
        grid=(heads,),
        in_specs=[
            pl.BlockSpec((count, 3 * HEAD), lambda head: (0, head)),
            pl.BlockSpec((count, HEAD), lambda head: (0, head)),
        ],
        out_specs=pl.BlockSpec((count, 3 * HEAD), lambda head: (0, head)),
        out_shape=jax.ShapeDtypeStruct(keyed.shape, jnp.bfloat16),
        compiler_params=pltpu.CompilerParams(vmem_limit_bytes=40 * 1024 * 1024),
        cost_estimate=pl.CostEstimate(
            flops=10 * heads * count * count * HEAD,
            bytes_accessed=14 * heads * count * HEAD,
            transcendentals=heads * count * count,
        ),
    )(keyed, head_grad)


def exchange(block, axis, flip):
    size = lax.axis_size(axis)
    return lax.ppermute(block, axis, [(i, i ^ flip) for i in range(size)])


def turn(block):
    pairs = [
        (g * 4 + z, SWAP[z] * 4 + SWAP[g]) for g in range(4) for z in range(4)
    ]
    return lax.ppermute(block, ("gy", "gz"), pairs)


def after(value, *earlier):
    return lax.optimization_barrier((value,) + earlier)[0]


def four_parts(block):
    opposite = exchange(block, "gy", 2)
    beside = exchange(block, "gy", 1)
    return block, beside, opposite, exchange(opposite, "gy", 1)


def both_halves(half):
    other = exchange(half, "gx", 1)
    first = lax.axis_index("gx") == 0
    return jnp.concatenate([jnp.where(first, half, other), jnp.where(first, other, half)], axis=0)


def local_columns(
    normed,
    out_grad,
    projected,
    mixed_heads,
    hidden_pre,
    attend_in,
    hidden_in,
    attend_out,
    hidden_out,
):
    side = lax.axis_index("gx")
    place = lax.axis_index("gy")
    deep = lax.axis_index("gz")
    column = 2 * lax.rem(deep, 2) + deep // 2
    half, block = normed.shape
    width = attend_in.shape[1]
    units = hidden_in.shape[1]

    grad_blocks = lax.all_gather(out_grad, "gz", axis=0)
    turned_out = turn(jnp.concatenate([hidden_out, attend_out], axis=0))
    grad_own = both_halves(out_grad)
    activated = gelu_value(hidden_pre.astype(jnp.float32)).astype(jnp.bfloat16)
    part_attend_out = jnp.einsum(
        "tg,td->gd", mixed_heads, grad_own, preferred_element_type=jnp.float32
    ).astype(jnp.bfloat16)
    part_hidden_out = jnp.einsum(
        "tg,td->gd", activated, grad_own, preferred_element_type=jnp.float32
    ).astype(jnp.bfloat16)

    normed_blocks = lax.all_gather(
        after(normed, grad_blocks, part_attend_out, part_hidden_out), "gz", axis=0
    )
    out_parts = four_parts(turned_out)
    in_block = jnp.concatenate([hidden_in, attend_in], axis=1)
    turned_in = turn(after(in_block, out_parts[2]))
    hidden_out_grad = lax.psum_scatter(
        after(part_hidden_out, normed_blocks), "gy", scatter_dimension=0, tiled=True
    )
    attend_out_grad = lax.psum_scatter(
        after(part_attend_out, hidden_out_grad), "gy", scatter_dimension=0, tiled=True
    )

    order = []
    for flip in range(4):
        slot = lax.bitwise_xor(place, flip)
        order.append(2 * lax.rem(slot, 2) + slot // 2)
    grad_slab = both_halves(
        jnp.concatenate(
            [lax.dynamic_index_in_dim(grad_blocks, at, 0, keepdims=False) for at in order], axis=1
        )
    )
    normed_slab = both_halves(jnp.concatenate([normed_blocks[at] for at in SWAP], axis=1))
    hidden_rows = jnp.concatenate([part[:units] for part in out_parts], axis=1)
    attend_rows = jnp.concatenate([part[units:] for part in out_parts], axis=1)

    pre_here = lax.dynamic_slice_in_dim(hidden_pre, column * units, units, 1)
    hidden_part = jnp.einsum(
        "td,gd->tg", grad_slab, hidden_rows, preferred_element_type=jnp.float32
    )
    hidden_grad = (hidden_part * gelu_slope(pre_here.astype(jnp.float32))).astype(jnp.bfloat16)
    part_hidden_in = jnp.einsum(
        "td,tq->dq", normed_slab, hidden_grad, preferred_element_type=jnp.float32
    ).astype(jnp.bfloat16)

    head_grad = jnp.einsum(
        "td,gd->tg", grad_slab, attend_rows, preferred_element_type=jnp.float32
    ).astype(jnp.bfloat16)
    keyed = lax.dynamic_slice_in_dim(projected, column * width, width, 1)
    projected_grad = attention_backward(keyed, head_grad)
    part_attend_in = jnp.einsum(
        "td,tq->dq", normed_slab, projected_grad, preferred_element_type=jnp.float32
    ).astype(jnp.bfloat16)

    hidden_in_sum = lax.psum_scatter(
        after(part_hidden_in, attend_out_grad, turned_in), "gy", scatter_dimension=0, tiled=True
    )
    attend_in_sum = lax.psum_scatter(
        after(part_attend_in, hidden_in_sum), "gy", scatter_dimension=0, tiled=True
    )
    hidden_in_grad = turn(hidden_in_sum)
    attend_in_grad = turn(attend_in_sum)

    in_parts = four_parts(turned_in)
    hidden_cols = jnp.concatenate([part[:, :units] for part in in_parts], axis=0)
    attend_cols = jnp.concatenate([part[:, units:] for part in in_parts], axis=0)

    def input_grad(start):
        attend_part = lax.dynamic_slice_in_dim(projected_grad, start, half, 0)
        hidden_part = lax.dynamic_slice_in_dim(hidden_grad, start, half, 0)
        return jnp.einsum(
            "tq,dq->td", attend_part, attend_cols, preferred_element_type=jnp.float32
        ) + jnp.einsum("tq,dq->td", hidden_part, hidden_cols, preferred_element_type=jnp.float32)

    arrived = exchange(input_grad((1 - side) * half).astype(jnp.bfloat16), "gx", 1)
    row_grad = (input_grad(side * half) + arrived.astype(jnp.float32)).astype(jnp.bfloat16)
    row_grad = jnp.concatenate(
        [
            lax.dynamic_slice_in_dim(
                row_grad, lax.bitwise_xor(place, SWAP[at]) * block, block, 1
            )
            for at in range(4)
        ],
        axis=1,
    )
    normed_grad = lax.psum_scatter(
        after(row_grad, attend_in_sum), "gz", scatter_dimension=1, tiled=True
    )
    return normed_grad, attend_in_grad, hidden_in_grad, attend_out_grad, hidden_out_grad


def chosen(*arrays):
    normed, projected, attend_in = arrays[0], arrays[2], arrays[5]
    sizes = tuple(lax.axis_size(axis) for axis in ("gx", "gy", "gz"))
    fits = (
        sizes == (2, 4, 4)
        and projected.shape[0] == LEN
        and attend_in.shape[1] % (3 * HEAD) == 0
        and normed.shape[0] * 2 == LEN
    )
    return (local_columns if fits else local)(*arrays)


def solution(mesh):
    placed = (
        P(("gy", "gx"), "gz"),
        P(("gy", "gx"), "gz"),
        P("gy", "gx"),
        P("gy", "gx"),
        P("gy", "gx"),
        P("gz", ("gx", "gy")),
        P("gz", ("gx", "gy")),
        P(("gx", "gy"), "gz"),
        P(("gx", "gy"), "gz"),
    )
    return jax.shard_map(
        chosen,
        mesh=mesh,
        in_specs=placed,
        out_specs=(
            P(("gy", "gx"), "gz"),
            P("gz", ("gx", "gy")),
            P("gz", ("gx", "gy")),
            P(("gx", "gy"), "gz"),
            P(("gx", "gy"), "gz"),
        ),
        check_vma=False,
    )
```

```python
import jax
import jax.numpy as jnp
from jax import lax
from jax.experimental import pallas as pl
from jax.experimental.pallas import tpu as pltpu
from jax.sharding import PartitionSpec as P

HEAD = 128
LEN = 1024


def gelu_value(values):
    return 0.5 * values * (1.0 + lax.erf(values * 0.7071067811865476))


def gelu_slope(values):
    return (
        0.5 * (1.0 + lax.erf(values * 0.7071067811865476))
        + values * jnp.exp(-0.5 * values * values) * 0.3989422804014327
    )


def local(
    normed,
    out_grad,
    projected,
    mixed_heads,
    hidden_pre,
    attend_in,
    hidden_in,
    attend_out,
    hidden_out,
):
    slab_count = projected.shape[0]
    depth = lax.axis_size("gz")
    block = slab_count // depth
    offset = lax.axis_index("gz") * block
    normed_slab, grad_slab = (
        lax.all_gather(normed, "gx", axis=0, tiled=True),
        lax.all_gather(out_grad, "gx", axis=0, tiled=True),
    )
    attend_cols, hidden_cols, attend_rows, hidden_rows = (
        lax.all_gather(attend_in, "gy", axis=1, tiled=True),
        lax.all_gather(hidden_in, "gy", axis=1, tiled=True),
        lax.all_gather(attend_out, "gy", axis=0, tiled=True),
        lax.all_gather(hidden_out, "gy", axis=0, tiled=True),
    )
    merge_part = jnp.einsum("td,gd->tg", grad_slab, attend_rows, preferred_element_type=jnp.float32)
    hidden_part = jnp.einsum(
        "td,gd->tg", grad_slab, hidden_rows, preferred_element_type=jnp.float32
    )
    pre_float = hidden_pre.astype(jnp.float32)
    merge_rows, hidden_sum = (
        lax.psum_scatter(merge_part, "gz", scatter_dimension=0, tiled=True),
        lax.psum_scatter(hidden_part, "gz", scatter_dimension=0, tiled=True),
    )
    slope_rows = gelu_slope(lax.dynamic_slice_in_dim(pre_float, offset, block, 0))
    hidden_grad_rows = (hidden_sum * slope_rows).astype(jnp.bfloat16)
    heads_grad = merge_rows.astype(jnp.bfloat16)
    heads_here = projected.shape[1] // (3 * HEAD)
    score_scale = HEAD ** (-0.5)
    span = max(block, LEN)
    keyed = projected.reshape(slab_count, heads_here, 3, HEAD)
    local_rows = lax.dynamic_slice_in_dim(keyed, offset, block, 0)
    queries = local_rows[:, :, 0]
    key_rows = keyed[:, :, 1]
    value_rows = keyed[:, :, 2]
    head_grad = heads_grad.reshape(block, heads_here, HEAD)
    scores = (
        jnp.einsum("qhd,khd->hqk", queries, key_rows, preferred_element_type=jnp.float32)
        * score_scale
    )
    largest = jnp.max(scores, axis=2, keepdims=True)
    weights = jnp.exp(scores - largest)
    probability = weights / jnp.sum(weights, axis=2, keepdims=True)
    value_grad = jnp.einsum(
        "hqk,qhd->khd",
        probability.astype(jnp.bfloat16),
        head_grad,
        preferred_element_type=jnp.float32,
    )
    prob_grad = jnp.einsum(
        "qhd,khd->hqk", head_grad, value_rows, preferred_element_type=jnp.float32
    )
    centre = jnp.sum(probability * prob_grad, axis=2, keepdims=True)
    score_grad = (probability * (prob_grad - centre)).astype(jnp.bfloat16)
    query_grad = score_scale * jnp.einsum(
        "hqk,khd->qhd", score_grad, key_rows, preferred_element_type=jnp.float32
    )
    key_grad = score_scale * jnp.einsum(
        "hqk,qhd->khd", score_grad, queries, preferred_element_type=jnp.float32
    )
    key_value = jnp.stack([key_grad, value_grad], axis=2).reshape(span, heads_here * 2 * HEAD)
    summed = (
        lax.psum_scatter(key_value.astype(jnp.bfloat16), "gz", scatter_dimension=0, tiled=True)
        .astype(jnp.float32)
        .reshape(block, heads_here, 2, HEAD)
    )
    projected_grad_rows = (
        jnp.concatenate([query_grad[:, :, None], summed], axis=2)
        .reshape(block, 3 * heads_here * HEAD)
        .astype(jnp.bfloat16)
    )
    projected_grad, hidden_grad = (
        lax.all_gather(projected_grad_rows, "gz", axis=0, tiled=True),
        lax.all_gather(hidden_grad_rows, "gz", axis=0, tiled=True),
    )
    local_grad = jnp.einsum(
        "tq,dq->td", projected_grad, attend_cols, preferred_element_type=jnp.float32
    ) + jnp.einsum("tq,dq->td", hidden_grad, hidden_cols, preferred_element_type=jnp.float32)
    normed_grad = lax.psum_scatter(
        local_grad.astype(jnp.bfloat16), "gx", scatter_dimension=0, tiled=True
    )
    activated = gelu_value(pre_float).astype(jnp.bfloat16)
    part_attend_in = jnp.einsum(
        "td,tq->dq", normed_slab, projected_grad, preferred_element_type=jnp.float32
    )
    part_hidden_in = jnp.einsum(
        "td,tq->dq", normed_slab, hidden_grad, preferred_element_type=jnp.float32
    )
    part_attend_out = jnp.einsum(
        "tg,td->gd", mixed_heads, grad_slab, preferred_element_type=jnp.float32
    )
    part_hidden_out = jnp.einsum(
        "tg,td->gd", activated, grad_slab, preferred_element_type=jnp.float32
    )
    sum_attend_in, sum_hidden_in, sum_attend_out, sum_hidden_out = (
        lax.psum_scatter(
            part_attend_in.astype(jnp.bfloat16), "gy", scatter_dimension=1, tiled=True
        ).astype(jnp.float32),
        lax.psum_scatter(
            part_hidden_in.astype(jnp.bfloat16), "gy", scatter_dimension=1, tiled=True
        ).astype(jnp.float32),
        lax.psum_scatter(
            part_attend_out.astype(jnp.bfloat16), "gy", scatter_dimension=0, tiled=True
        ).astype(jnp.float32),
        lax.psum_scatter(
            part_hidden_out.astype(jnp.bfloat16), "gy", scatter_dimension=0, tiled=True
        ).astype(jnp.float32),
    )
    return (
        normed_grad,
        sum_attend_in.astype(jnp.bfloat16),
        sum_hidden_in.astype(jnp.bfloat16),
        sum_attend_out.astype(jnp.bfloat16),
        sum_hidden_out.astype(jnp.bfloat16),
    )


SWAP = (0, 2, 1, 3)


def attention_kernel(keyed_ref, grad_ref, out_ref):
    score_scale = HEAD ** (-0.5)
    across = (((1,), (1,)), ((), ()))
    along = (((0,), (0,)), ((), ()))
    keys = keyed_ref[:, HEAD : 2 * HEAD]
    values = keyed_ref[:, 2 * HEAD :]
    count = keyed_ref.shape[0]
    step = min(256, count)
    key_grad = jnp.zeros((count, HEAD), jnp.float32)
    value_grad = jnp.zeros((count, HEAD), jnp.float32)
    for start in range(0, count, step):
        rows = slice(start, start + step)
        queries = keyed_ref[rows, :HEAD]
        grads = grad_ref[rows, :]
        scores = (
            lax.dot_general(queries, keys, across, preferred_element_type=jnp.float32)
            * score_scale
        )
        weights = jnp.exp(scores - jnp.max(scores, axis=1, keepdims=True))
        probability = weights / jnp.sum(weights, axis=1, keepdims=True)
        prob_grad = lax.dot_general(grads, values, across, preferred_element_type=jnp.float32)
        centre = jnp.sum(probability * prob_grad, axis=1, keepdims=True)
        score_grad = (probability * (prob_grad - centre)).astype(jnp.bfloat16)
        query_grad = score_scale * jnp.dot(score_grad, keys, preferred_element_type=jnp.float32)
        out_ref[rows, :HEAD] = query_grad.astype(jnp.bfloat16)
        key_grad += lax.dot_general(
            score_grad, queries, along, preferred_element_type=jnp.float32
        )
        value_grad += lax.dot_general(
            probability.astype(jnp.bfloat16), grads, along, preferred_element_type=jnp.float32
        )
    out_ref[:, HEAD : 2 * HEAD] = (score_scale * key_grad).astype(jnp.bfloat16)
    out_ref[:, 2 * HEAD :] = value_grad.astype(jnp.bfloat16)


def attention_backward(keyed, head_grad):
    count = keyed.shape[0]
    heads = keyed.shape[1] // (3 * HEAD)
    return pl.pallas_call(
        attention_kernel,
        grid=(heads,),
        in_specs=[
            pl.BlockSpec((count, 3 * HEAD), lambda head: (0, head)),
            pl.BlockSpec((count, HEAD), lambda head: (0, head)),
        ],
        out_specs=pl.BlockSpec((count, 3 * HEAD), lambda head: (0, head)),
        out_shape=jax.ShapeDtypeStruct(keyed.shape, jnp.bfloat16),
        compiler_params=pltpu.CompilerParams(vmem_limit_bytes=40 * 1024 * 1024),
        cost_estimate=pl.CostEstimate(
            flops=10 * heads * count * count * HEAD,
            bytes_accessed=14 * heads * count * HEAD,
            transcendentals=heads * count * count,
        ),
    )(keyed, head_grad)


def exchange(block, axis, flip):
    size = lax.axis_size(axis)
    return lax.ppermute(block, axis, [(i, i ^ flip) for i in range(size)])


def turn(block):
    pairs = [
        (g * 4 + z, SWAP[z] * 4 + SWAP[g]) for g in range(4) for z in range(4)
    ]
    return lax.ppermute(block, ("gy", "gz"), pairs)


def after(value, *earlier):
    return lax.optimization_barrier((value,) + earlier)[0]


def at_place(parts, index, axis):
    taken = [lax.dynamic_index_in_dim(part, index, axis, keepdims=False) for part in parts]
    return taken[0] if len(taken) == 1 else jnp.concatenate(taken, axis=taken[0].ndim - 2)


def add(left, right):
    return (left.astype(jnp.float32) + right.astype(jnp.float32)).astype(jnp.bfloat16)


def pair_sum(parts):
    core = lax.rem(lax.axis_index("gy"), 2)
    pairs = [part.reshape(2, 2, part.shape[0] // 4, part.shape[1]) for part in parts]
    arrived = exchange(at_place(pairs, 1 - core, 1), "gy", 1)
    return add(at_place(pairs, core, 1), arrived)


def far_sum(pair, *earlier):
    row = lax.axis_index("gy") // 2
    sent = lax.dynamic_index_in_dim(pair, 1 - row, 0, keepdims=False)
    arrived = exchange(after(sent, *earlier) if earlier else sent, "gy", 2)
    return add(lax.dynamic_index_in_dim(pair, row, 0, keepdims=False), arrived)


def four_parts(block, *earlier):
    opposite = exchange(after(block, *earlier), "gy", 2)
    beside = exchange(block, "gy", 1)
    return block, beside, opposite, exchange(opposite, "gy", 1)


def both_halves(half):
    other = exchange(half, "gx", 1)
    first = lax.axis_index("gx") == 0
    return jnp.concatenate([jnp.where(first, half, other), jnp.where(first, other, half)], axis=0)


def local_columns(
    normed,
    out_grad,
    projected,
    mixed_heads,
    hidden_pre,
    attend_in,
    hidden_in,
    attend_out,
    hidden_out,
):
    side = lax.axis_index("gx")
    place = lax.axis_index("gy")
    deep = lax.axis_index("gz")
    column = 2 * lax.rem(deep, 2) + deep // 2
    half, block = normed.shape
    width = attend_in.shape[1]
    units = hidden_in.shape[1]

    grad_blocks = lax.all_gather(out_grad, "gz", axis=0)
    out_block = jnp.concatenate([hidden_out, attend_out], axis=0)
    turned_out = turn(after(out_block, grad_blocks))
    grad_own = both_halves(out_grad)
    activated = gelu_value(hidden_pre.astype(jnp.float32)).astype(jnp.bfloat16)
    part_attend_out = jnp.einsum(
        "tg,td->gd", mixed_heads, grad_own, preferred_element_type=jnp.float32
    ).astype(jnp.bfloat16)
    part_hidden_out = jnp.einsum(
        "tg,td->gd", activated, grad_own, preferred_element_type=jnp.float32
    ).astype(jnp.bfloat16)
    out_sum = far_sum(pair_sum([part_hidden_out, part_attend_out]))
    hidden_out_grad, attend_out_grad = out_sum[:units], out_sum[units:]

    order = []
    for flip in range(4):
        slot = lax.bitwise_xor(place, flip)
        order.append(2 * lax.rem(slot, 2) + slot // 2)
    grad_slab = both_halves(
        jnp.concatenate(
            [lax.dynamic_index_in_dim(grad_blocks, at, 0, keepdims=False) for at in order], axis=1
        )
    )
    out_parts = four_parts(turned_out, out_sum, grad_slab)
    normed_blocks = lax.all_gather(after(normed, turned_out, grad_slab), "gz", axis=0)
    in_block = jnp.concatenate([hidden_in, attend_in], axis=1)
    turned_in = turn(after(in_block, out_parts[2]))
    normed_slab = both_halves(jnp.concatenate([normed_blocks[at] for at in SWAP], axis=1))
    hidden_rows = jnp.concatenate([part[:units] for part in out_parts], axis=1)
    attend_rows = jnp.concatenate([part[units:] for part in out_parts], axis=1)

    pre_here = lax.dynamic_slice_in_dim(hidden_pre, column * units, units, 1)
    hidden_part = jnp.einsum(
        "td,gd->tg", grad_slab, hidden_rows, preferred_element_type=jnp.float32
    )
    hidden_grad = (hidden_part * gelu_slope(pre_here.astype(jnp.float32))).astype(jnp.bfloat16)
    part_hidden_in = jnp.einsum(
        "td,tq->dq", normed_slab, after(hidden_grad, turned_in), preferred_element_type=jnp.float32
    ).astype(jnp.bfloat16)

    head_grad = jnp.einsum(
        "td,gd->tg", grad_slab, attend_rows, preferred_element_type=jnp.float32
    ).astype(jnp.bfloat16)
    keyed = lax.dynamic_slice_in_dim(projected, column * width, width, 1)
    projected_grad = attention_backward(keyed, head_grad)
    part_attend_in = jnp.einsum(
        "td,tq->dq", normed_slab, projected_grad, preferred_element_type=jnp.float32
    ).astype(jnp.bfloat16)

    hidden_in_sum = far_sum(pair_sum([part_hidden_in]))
    hidden_in_grad = turn(hidden_in_sum)
    far_in = exchange(after(turned_in, hidden_in_sum), "gy", 2)
    in_parts = (
        turned_in,
        exchange(turned_in, "gy", 1),
        far_in,
        exchange(after(far_in, hidden_in_grad), "gy", 1),
    )
    attend_in_sum = far_sum(pair_sum([part_attend_in]), in_parts[2])
    attend_in_grad = turn(attend_in_sum)
    hidden_cols = jnp.concatenate([part[:, :units] for part in in_parts], axis=0)
    attend_cols = jnp.concatenate([part[:, units:] for part in in_parts], axis=0)

    def input_grad(start):
        attend_part = lax.dynamic_slice_in_dim(projected_grad, start, half, 0)
        hidden_part = lax.dynamic_slice_in_dim(hidden_grad, start, half, 0)
        return jnp.einsum(
            "tq,dq->td", attend_part, attend_cols, preferred_element_type=jnp.float32
        ) + jnp.einsum("tq,dq->td", hidden_part, hidden_cols, preferred_element_type=jnp.float32)

    leaving = input_grad((1 - side) * half).astype(jnp.bfloat16)
    arrived = exchange(leaving, "gx", 1)
    row_grad = (input_grad(side * half) + arrived.astype(jnp.float32)).astype(jnp.bfloat16)
    row_grad = jnp.concatenate(
        [
            lax.dynamic_slice_in_dim(
                row_grad, lax.bitwise_xor(place, SWAP[at]) * block, block, 1
            )
            for at in range(4)
        ],
        axis=1,
    )
    normed_grad = lax.psum_scatter(
        after(row_grad, attend_in_grad), "gz", scatter_dimension=1, tiled=True
    )
    return normed_grad, attend_in_grad, hidden_in_grad, attend_out_grad, hidden_out_grad


def chosen(*arrays):
    normed, projected, attend_in = arrays[0], arrays[2], arrays[5]
    sizes = tuple(lax.axis_size(axis) for axis in ("gx", "gy", "gz"))
    fits = (
        sizes == (2, 4, 4)
        and projected.shape[0] == LEN
        and attend_in.shape[1] % (3 * HEAD) == 0
        and normed.shape[0] * 2 == LEN
    )
    return (local_columns if fits else local)(*arrays)


def solution(mesh):
    placed = (
        P(("gy", "gx"), "gz"),
        P(("gy", "gx"), "gz"),
        P("gy", "gx"),
        P("gy", "gx"),
        P("gy", "gx"),
        P("gz", ("gx", "gy")),
        P("gz", ("gx", "gy")),
        P(("gx", "gy"), "gz"),
        P(("gx", "gy"), "gz"),
    )
    return jax.shard_map(
        chosen,
        mesh=mesh,
        in_specs=placed,
        out_specs=(
            P(("gy", "gx"), "gz"),
            P("gz", ("gx", "gy")),
            P("gz", ("gx", "gy")),
            P(("gx", "gy"), "gz"),
            P(("gx", "gy"), "gz"),
        ),
        check_vma=False,
    )
```

```python
import jax
import jax.numpy as jnp
from jax import lax
from jax.experimental import pallas as pl
from jax.experimental.pallas import tpu as pltpu
from jax.sharding import PartitionSpec as P

HEAD = 128
LEN = 1024


def gelu_value(values):
    return 0.5 * values * (1.0 + lax.erf(values * 0.7071067811865476))


def gelu_slope(values):
    return (
        0.5 * (1.0 + lax.erf(values * 0.7071067811865476))
        + values * jnp.exp(-0.5 * values * values) * 0.3989422804014327
    )


def local(
    normed,
    out_grad,
    projected,
    mixed_heads,
    hidden_pre,
    attend_in,
    hidden_in,
    attend_out,
    hidden_out,
):
    slab_count = projected.shape[0]
    depth = lax.axis_size("gz")
    block = slab_count // depth
    offset = lax.axis_index("gz") * block
    normed_slab, grad_slab = (
        lax.all_gather(normed, "gx", axis=0, tiled=True),
        lax.all_gather(out_grad, "gx", axis=0, tiled=True),
    )
    attend_cols, hidden_cols, attend_rows, hidden_rows = (
        lax.all_gather(attend_in, "gy", axis=1, tiled=True),
        lax.all_gather(hidden_in, "gy", axis=1, tiled=True),
        lax.all_gather(attend_out, "gy", axis=0, tiled=True),
        lax.all_gather(hidden_out, "gy", axis=0, tiled=True),
    )
    merge_part = jnp.einsum("td,gd->tg", grad_slab, attend_rows, preferred_element_type=jnp.float32)
    hidden_part = jnp.einsum(
        "td,gd->tg", grad_slab, hidden_rows, preferred_element_type=jnp.float32
    )
    pre_float = hidden_pre.astype(jnp.float32)
    merge_rows, hidden_sum = (
        lax.psum_scatter(merge_part, "gz", scatter_dimension=0, tiled=True),
        lax.psum_scatter(hidden_part, "gz", scatter_dimension=0, tiled=True),
    )
    slope_rows = gelu_slope(lax.dynamic_slice_in_dim(pre_float, offset, block, 0))
    hidden_grad_rows = (hidden_sum * slope_rows).astype(jnp.bfloat16)
    heads_grad = merge_rows.astype(jnp.bfloat16)
    heads_here = projected.shape[1] // (3 * HEAD)
    score_scale = HEAD ** (-0.5)
    span = max(block, LEN)
    keyed = projected.reshape(slab_count, heads_here, 3, HEAD)
    local_rows = lax.dynamic_slice_in_dim(keyed, offset, block, 0)
    queries = local_rows[:, :, 0]
    key_rows = keyed[:, :, 1]
    value_rows = keyed[:, :, 2]
    head_grad = heads_grad.reshape(block, heads_here, HEAD)
    scores = (
        jnp.einsum("qhd,khd->hqk", queries, key_rows, preferred_element_type=jnp.float32)
        * score_scale
    )
    largest = jnp.max(scores, axis=2, keepdims=True)
    weights = jnp.exp(scores - largest)
    probability = weights / jnp.sum(weights, axis=2, keepdims=True)
    value_grad = jnp.einsum(
        "hqk,qhd->khd",
        probability.astype(jnp.bfloat16),
        head_grad,
        preferred_element_type=jnp.float32,
    )
    prob_grad = jnp.einsum(
        "qhd,khd->hqk", head_grad, value_rows, preferred_element_type=jnp.float32
    )
    centre = jnp.sum(probability * prob_grad, axis=2, keepdims=True)
    score_grad = (probability * (prob_grad - centre)).astype(jnp.bfloat16)
    query_grad = score_scale * jnp.einsum(
        "hqk,khd->qhd", score_grad, key_rows, preferred_element_type=jnp.float32
    )
    key_grad = score_scale * jnp.einsum(
        "hqk,qhd->khd", score_grad, queries, preferred_element_type=jnp.float32
    )
    key_value = jnp.stack([key_grad, value_grad], axis=2).reshape(span, heads_here * 2 * HEAD)
    summed = (
        lax.psum_scatter(key_value.astype(jnp.bfloat16), "gz", scatter_dimension=0, tiled=True)
        .astype(jnp.float32)
        .reshape(block, heads_here, 2, HEAD)
    )
    projected_grad_rows = (
        jnp.concatenate([query_grad[:, :, None], summed], axis=2)
        .reshape(block, 3 * heads_here * HEAD)
        .astype(jnp.bfloat16)
    )
    projected_grad, hidden_grad = (
        lax.all_gather(projected_grad_rows, "gz", axis=0, tiled=True),
        lax.all_gather(hidden_grad_rows, "gz", axis=0, tiled=True),
    )
    local_grad = jnp.einsum(
        "tq,dq->td", projected_grad, attend_cols, preferred_element_type=jnp.float32
    ) + jnp.einsum("tq,dq->td", hidden_grad, hidden_cols, preferred_element_type=jnp.float32)
    normed_grad = lax.psum_scatter(
        local_grad.astype(jnp.bfloat16), "gx", scatter_dimension=0, tiled=True
    )
    activated = gelu_value(pre_float).astype(jnp.bfloat16)
    part_attend_in = jnp.einsum(
        "td,tq->dq", normed_slab, projected_grad, preferred_element_type=jnp.float32
    )
    part_hidden_in = jnp.einsum(
        "td,tq->dq", normed_slab, hidden_grad, preferred_element_type=jnp.float32
    )
    part_attend_out = jnp.einsum(
        "tg,td->gd", mixed_heads, grad_slab, preferred_element_type=jnp.float32
    )
    part_hidden_out = jnp.einsum(
        "tg,td->gd", activated, grad_slab, preferred_element_type=jnp.float32
    )
    sum_attend_in, sum_hidden_in, sum_attend_out, sum_hidden_out = (
        lax.psum_scatter(
            part_attend_in.astype(jnp.bfloat16), "gy", scatter_dimension=1, tiled=True
        ).astype(jnp.float32),
        lax.psum_scatter(
            part_hidden_in.astype(jnp.bfloat16), "gy", scatter_dimension=1, tiled=True
        ).astype(jnp.float32),
        lax.psum_scatter(
            part_attend_out.astype(jnp.bfloat16), "gy", scatter_dimension=0, tiled=True
        ).astype(jnp.float32),
        lax.psum_scatter(
            part_hidden_out.astype(jnp.bfloat16), "gy", scatter_dimension=0, tiled=True
        ).astype(jnp.float32),
    )
    return (
        normed_grad,
        sum_attend_in.astype(jnp.bfloat16),
        sum_hidden_in.astype(jnp.bfloat16),
        sum_attend_out.astype(jnp.bfloat16),
        sum_hidden_out.astype(jnp.bfloat16),
    )


SWAP = (0, 2, 1, 3)


def attention_kernel(keyed_ref, grad_ref, out_ref):
    score_scale = HEAD ** (-0.5)
    across = (((1,), (1,)), ((), ()))
    along = (((0,), (0,)), ((), ()))
    keys = keyed_ref[:, HEAD : 2 * HEAD]
    values = keyed_ref[:, 2 * HEAD :]
    count = keyed_ref.shape[0]
    step = min(256, count)
    key_grad = jnp.zeros((count, HEAD), jnp.float32)
    value_grad = jnp.zeros((count, HEAD), jnp.float32)
    for start in range(0, count, step):
        rows = slice(start, start + step)
        queries = keyed_ref[rows, :HEAD]
        grads = grad_ref[rows, :]
        scores = (
            lax.dot_general(queries, keys, across, preferred_element_type=jnp.float32)
            * score_scale
        )
        weights = jnp.exp(scores - jnp.max(scores, axis=1, keepdims=True))
        probability = weights / jnp.sum(weights, axis=1, keepdims=True)
        prob_grad = lax.dot_general(grads, values, across, preferred_element_type=jnp.float32)
        centre = jnp.sum(probability * prob_grad, axis=1, keepdims=True)
        score_grad = (probability * (prob_grad - centre)).astype(jnp.bfloat16)
        query_grad = score_scale * jnp.dot(score_grad, keys, preferred_element_type=jnp.float32)
        out_ref[rows, :HEAD] = query_grad.astype(jnp.bfloat16)
        key_grad += lax.dot_general(
            score_grad, queries, along, preferred_element_type=jnp.float32
        )
        value_grad += lax.dot_general(
            probability.astype(jnp.bfloat16), grads, along, preferred_element_type=jnp.float32
        )
    out_ref[:, HEAD : 2 * HEAD] = (score_scale * key_grad).astype(jnp.bfloat16)
    out_ref[:, 2 * HEAD :] = value_grad.astype(jnp.bfloat16)


def attention_backward(keyed, head_grad):
    count = keyed.shape[0]
    heads = keyed.shape[1] // (3 * HEAD)
    return pl.pallas_call(
        attention_kernel,
        grid=(heads,),
        in_specs=[
            pl.BlockSpec((count, 3 * HEAD), lambda head: (0, head)),
            pl.BlockSpec((count, HEAD), lambda head: (0, head)),
        ],
        out_specs=pl.BlockSpec((count, 3 * HEAD), lambda head: (0, head)),
        out_shape=jax.ShapeDtypeStruct(keyed.shape, jnp.bfloat16),
        compiler_params=pltpu.CompilerParams(vmem_limit_bytes=40 * 1024 * 1024),
        cost_estimate=pl.CostEstimate(
            flops=10 * heads * count * count * HEAD,
            bytes_accessed=14 * heads * count * HEAD,
            transcendentals=heads * count * count,
        ),
    )(keyed, head_grad)


def exchange(block, axis, flip):
    size = lax.axis_size(axis)
    return lax.ppermute(block, axis, [(i, i ^ flip) for i in range(size)])


def turn(block):
    pairs = [
        (g * 4 + z, SWAP[z] * 4 + SWAP[g]) for g in range(4) for z in range(4)
    ]
    return lax.ppermute(block, ("gy", "gz"), pairs)


def after(value, *earlier):
    return lax.optimization_barrier((value,) + earlier)[0]


def at_place(parts, index, axis):
    taken = [lax.dynamic_index_in_dim(part, index, axis, keepdims=False) for part in parts]
    return taken[0] if len(taken) == 1 else jnp.concatenate(taken, axis=taken[0].ndim - 2)


def add(left, right):
    return (left.astype(jnp.float32) + right.astype(jnp.float32)).astype(jnp.bfloat16)


def pair_sum(parts):
    core = lax.rem(lax.axis_index("gy"), 2)
    pairs = [part.reshape(2, 2, part.shape[0] // 4, part.shape[1]) for part in parts]
    arrived = exchange(at_place(pairs, 1 - core, 1), "gy", 1)
    return add(at_place(pairs, core, 1), arrived)


def far_sum(pair, *earlier):
    row = lax.axis_index("gy") // 2
    sent = lax.dynamic_index_in_dim(pair, 1 - row, 0, keepdims=False)
    arrived = exchange(after(sent, *earlier) if earlier else sent, "gy", 2)
    return add(lax.dynamic_index_in_dim(pair, row, 0, keepdims=False), arrived)


def four_parts(block):
    opposite = exchange(block, "gy", 2)
    beside = exchange(block, "gy", 1)
    return block, beside, opposite, exchange(opposite, "gy", 1)


def both_halves(half):
    other = exchange(half, "gx", 1)
    first = lax.axis_index("gx") == 0
    return jnp.concatenate([jnp.where(first, half, other), jnp.where(first, other, half)], axis=0)


def local_columns(
    normed,
    out_grad,
    projected,
    mixed_heads,
    hidden_pre,
    attend_in,
    hidden_in,
    attend_out,
    hidden_out,
):
    side = lax.axis_index("gx")
    place = lax.axis_index("gy")
    deep = lax.axis_index("gz")
    column = 2 * lax.rem(deep, 2) + deep // 2
    half, block = normed.shape
    width = attend_in.shape[1]
    units = hidden_in.shape[1]

    grad_blocks = lax.all_gather(out_grad, "gz", axis=0)
    out_block = jnp.concatenate([hidden_out, attend_out], axis=0)
    turned_out = turn(out_block)
    grad_own = both_halves(out_grad)
    activated = gelu_value(hidden_pre.astype(jnp.float32)).astype(jnp.bfloat16)
    part_attend_out = jnp.einsum(
        "tg,td->gd", mixed_heads, grad_own, preferred_element_type=jnp.float32
    ).astype(jnp.bfloat16)
    part_hidden_out = jnp.einsum(
        "tg,td->gd", activated, grad_own, preferred_element_type=jnp.float32
    ).astype(jnp.bfloat16)

    order = []
    for flip in range(4):
        slot = lax.bitwise_xor(place, flip)
        order.append(2 * lax.rem(slot, 2) + slot // 2)
    grad_slab = both_halves(
        jnp.concatenate(
            [lax.dynamic_index_in_dim(grad_blocks, at, 0, keepdims=False) for at in order], axis=1
        )
    )
    out_parts = four_parts(turned_out)
    out_sum = far_sum(pair_sum([part_hidden_out, part_attend_out]), out_parts[2])
    hidden_out_grad, attend_out_grad = out_sum[:units], out_sum[units:]
    normed_blocks = lax.all_gather(after(normed, grad_blocks, part_attend_out, part_hidden_out), "gz", axis=0)
    in_block = jnp.concatenate([hidden_in, attend_in], axis=1)
    turned_in = turn(after(in_block, out_parts[2]))
    normed_slab = both_halves(
        after(jnp.concatenate([normed_blocks[at] for at in SWAP], axis=1), grad_slab)
    )
    hidden_rows = jnp.concatenate([part[:units] for part in out_parts], axis=1)
    attend_rows = jnp.concatenate([part[units:] for part in out_parts], axis=1)

    pre_here = lax.dynamic_slice_in_dim(hidden_pre, column * units, units, 1)
    hidden_part = jnp.einsum(
        "td,gd->tg", grad_slab, hidden_rows, preferred_element_type=jnp.float32
    )
    hidden_grad = (hidden_part * gelu_slope(pre_here.astype(jnp.float32))).astype(jnp.bfloat16)
    part_hidden_in = jnp.einsum(
        "td,tq->dq", normed_slab, after(hidden_grad, turned_in), preferred_element_type=jnp.float32
    ).astype(jnp.bfloat16)

    head_grad = jnp.einsum(
        "td,gd->tg", grad_slab, attend_rows, preferred_element_type=jnp.float32
    ).astype(jnp.bfloat16)
    keyed = lax.dynamic_slice_in_dim(projected, column * width, width, 1)
    projected_grad = attention_backward(keyed, head_grad)
    part_attend_in = jnp.einsum(
        "td,tq->dq", normed_slab, projected_grad, preferred_element_type=jnp.float32
    ).astype(jnp.bfloat16)

    hidden_in_sum = far_sum(pair_sum([part_hidden_in]), out_sum)
    hidden_in_grad = turn(hidden_in_sum)
    in_parts = four_parts(turned_in)
    attend_in_sum = far_sum(pair_sum([part_attend_in]), in_parts[2])
    attend_in_grad = turn(attend_in_sum)
    hidden_cols = jnp.concatenate([part[:, :units] for part in in_parts], axis=0)
    attend_cols = jnp.concatenate([part[:, units:] for part in in_parts], axis=0)

    def input_grad(start):
        attend_part = lax.dynamic_slice_in_dim(projected_grad, start, half, 0)
        hidden_part = lax.dynamic_slice_in_dim(hidden_grad, start, half, 0)
        return jnp.einsum(
            "tq,dq->td", attend_part, attend_cols, preferred_element_type=jnp.float32
        ) + jnp.einsum("tq,dq->td", hidden_part, hidden_cols, preferred_element_type=jnp.float32)

    leaving = input_grad((1 - side) * half).astype(jnp.bfloat16)
    arrived = exchange(leaving, "gx", 1)
    row_grad = (input_grad(side * half) + arrived.astype(jnp.float32)).astype(jnp.bfloat16)
    row_grad = jnp.concatenate(
        [
            lax.dynamic_slice_in_dim(
                row_grad, lax.bitwise_xor(place, SWAP[at]) * block, block, 1
            )
            for at in range(4)
        ],
        axis=1,
    )
    normed_grad = lax.psum_scatter(
        after(row_grad, hidden_in_grad), "gz", scatter_dimension=1, tiled=True
    )
    return normed_grad, attend_in_grad, hidden_in_grad, attend_out_grad, hidden_out_grad


def chosen(*arrays):
    normed, projected, attend_in = arrays[0], arrays[2], arrays[5]
    sizes = tuple(lax.axis_size(axis) for axis in ("gx", "gy", "gz"))
    fits = (
        sizes == (2, 4, 4)
        and projected.shape[0] == LEN
        and attend_in.shape[1] % (3 * HEAD) == 0
        and normed.shape[0] * 2 == LEN
    )
    return (local_columns if fits else local)(*arrays)


def solution(mesh):
    placed = (
        P(("gy", "gx"), "gz"),
        P(("gy", "gx"), "gz"),
        P("gy", "gx"),
        P("gy", "gx"),
        P("gy", "gx"),
        P("gz", ("gx", "gy")),
        P("gz", ("gx", "gy")),
        P(("gx", "gy"), "gz"),
        P(("gx", "gy"), "gz"),
    )
    return jax.shard_map(
        chosen,
        mesh=mesh,
        in_specs=placed,
        out_specs=(
            P(("gy", "gx"), "gz"),
            P("gz", ("gx", "gy")),
            P("gz", ("gx", "gy")),
            P(("gx", "gy"), "gz"),
            P(("gx", "gy"), "gz"),
        ),
        check_vma=False,
    )
```
